32 devices in a mesh: dp: 4 (over z), mp: 2 (over y), expert: 4 (over x, core).
Axes of the slice: x: 2, y: 2, z: 4, core: 2. Of those that a mesh axis runs over, the one named last changes fastest.
Arguments:
- attn_out: bfloat16 [1024, 2304], P('dp', 'mp'), may hold values from -6 to 6
- residual: float32 [1024, 2304], P(('dp', 'mp', 'expert'))
- proj_weight: bfloat16 [2304, 2304], P('mp'), may hold values from -0.125 to 0.125
- norm_gain: float32 [2304], replicated, may hold values from 0.1 to 1.9
- gate_weight: bfloat16 [8, 2304, 4096], P('mp', None, 'expert'), may hold values from -0.125 to 0.125
- up_weight: bfloat16 [8, 2304, 4096], P('mp', None, 'expert'), may hold values from -0.125 to 0.125
- down_weight: bfloat16 [8, 4096, 2304], P('mp', 'expert'), may hold values from -0.09375 to 0.09375
- routes: int32 [1024, 2], P(('dp', 'mp', 'expert')), may hold values from 0 to 7, as said below
- route_weights: float32 [1024, 2], P(('dp', 'mp', 'expert')), may hold values from 0.2 to 1
Outputs:
- mixed: float32 [1024, 2304], P(('dp', 'mp', 'expert'))
The draws below stay inside these ranges and needn't reach their ends.
Inputs may be any that keep to these rules, and one draw needn't show every extreme that they name: `routes`: the two ids of a row differ. In the rows of each device (aligned blocks of 32 rows, in order) every expert is named by at most 16 rows; one expert, the same in all blocks, is named by exactly 16 rows in every block, and the other 48 names of a block are spread as evenly as possible over the other experts.
All inputs are finite; a program needn't handle non-finite values.
Results may differ from the reference program's by a relative error of at most 0.0015.
Values may be sent and summed in bfloat16 or wider, within the bound.
A program may use at most 128 MiB of HBM per device.

```python
import math
import jax
import jax.numpy as jnp
from jax import lax

D = 2304
FF = 4096
EXPERTS = 8
ROWS = 32
MOST = 16
UNITS_DEV = 1024
TOKENS = 1024
N_EXPERT = 4


def draw_residual(key, part):
    noise_key, row_key, column_key = jax.random.split(key, 3)
    columns = jnp.arange(D, dtype=jnp.float32) / D
    noise = jax.random.normal(noise_key, (TOKENS, D), jnp.float32)
    row_scale = jnp.exp(jax.random.uniform(row_key, (TOKENS, 1), jnp.float32, 0.0, math.log(10.0)))
    column_scale = jnp.exp(columns * math.log(10.0) + jax.random.uniform(column_key, (1, D), jnp.float32, math.log(0.7), math.log(1.4)))
    return (0.1 * noise * row_scale * column_scale).astype(jnp.float32)


def draw_routes(key, part):
    block_total = TOKENS // ROWS
    hot_key, order_key, row_key = jax.random.split(key, 3)
    hottest = jax.random.randint(hot_key, (), 0, EXPERTS).astype(jnp.int32)
    order_keys = jax.random.split(order_key, block_total)
    row_keys = jax.random.split(row_key, block_total)
    other_count = EXPERTS - 1
    remain = 2 * ROWS - MOST
    even_share = remain // other_count
    leftover = remain % other_count
    counts = jnp.concatenate([jnp.array([MOST], jnp.int32), (even_share + (jnp.arange(other_count) < leftover)).astype(jnp.int32)])
    bounds = jnp.cumsum(counts)
    positions = jnp.arange(2 * ROWS, dtype=jnp.int32)
    segment = jnp.sum((positions[:, None] >= bounds[None, :]).astype(jnp.int32), axis=1)

    def one_block(order_seed, row_seed):
        others = (hottest + 1 + jax.random.permutation(order_seed, other_count).astype(jnp.int32)) % EXPERTS
        ordering = jnp.concatenate([hottest[None], others])
        sequence = ordering[segment]
        shuffle = jax.random.permutation(row_seed, ROWS).astype(jnp.int32)
        return jnp.stack([sequence[shuffle], sequence[shuffle + ROWS]], axis=1)
    return jax.vmap(one_block)(order_keys, row_keys).reshape(TOKENS, 2).astype(jnp.int32)


def shard_levels(key, shape, pieces, low, largest):
    def one(axis_at, parts):
        steps = jax.random.uniform(jax.random.fold_in(jax.random.fold_in(key, 6), axis_at), (parts,), jnp.float32, low / len(pieces), largest / len(pieces))
        return jnp.repeat(jnp.exp(steps), shape[axis_at] // parts).reshape((-1,) + (1,) * (len(shape) - axis_at - 1))

    factor_of = one(*pieces[0])
    for cut in pieces[1:]:
        factor_of = factor_of * one(*cut)
    return factor_of


def normal_values(own_key, dims, scale, most, pieces=(), kind=jnp.bfloat16):
    loudness = shard_levels(own_key, dims, pieces, -0.22, 0.18) if pieces else 1.0
    result = jax.random.normal(own_key, dims, jnp.float32) * scale * loudness
    return jnp.minimum(jnp.maximum(result, -most), most).astype(kind)


def setup_inputs(seed: int = 0) -> dict:
    key_list = jax.random.split(jax.random.key(seed), 10)
    return {
        "attn_out": normal_values(key_list[0], (TOKENS, D), 1.0, 6.0, ((0, 4), (1, 2))),
        "residual": draw_residual(jax.random.fold_in(key_list[9], 71), 0),
        "proj_weight": normal_values(key_list[2], (D, D), D ** -0.5, 0.125, ((0, 2),)),
        "norm_gain": jnp.clip(1.0 + 0.18 * jax.random.normal(key_list[3], (D,), jnp.float32), 0.1, 1.9),
        "gate_weight": normal_values(key_list[4], (EXPERTS, D, FF), D ** -0.5, 0.125, ((0, 2), (2, 4))),
        "up_weight": normal_values(key_list[5], (EXPERTS, D, FF), D ** -0.5, 0.125, ((0, 2), (2, 4))),
        "down_weight": normal_values(key_list[6], (EXPERTS, FF, D), FF ** -0.5, 0.09375, ((0, 2), (1, 4))),
        "routes": draw_routes(jax.random.fold_in(key_list[9], 71), 0),
        "route_weights": jnp.clip(0.2 + 0.8 * jax.random.uniform(key_list[8], (TOKENS, 2), jnp.float32) ** shard_levels(key_list[8], (TOKENS, 2), ((0, 32),), -0.2, 0.2), 0.2, 1.0),
    }


EPSILON = 1e-06

def reference(attn_out, residual, proj_weight, norm_gain, gate_weight, up_weight, down_weight, routes, route_weights):
    projected = jnp.dot(attn_out, proj_weight, preferred_element_type=jnp.float32)
    hidden_state = residual + projected
    inverse_rms = lax.rsqrt(lax.optimization_barrier(jnp.mean(hidden_state * hidden_state, axis=1, keepdims=True)) + EPSILON)
    normed = (hidden_state * inverse_rms * norm_gain).astype(jnp.bfloat16)
    capacity = MOST * (TOKENS // ROWS)
    expert_ids = routes.reshape(-1)
    collected = jnp.zeros((TOKENS * 2, D), jnp.float32)
    for expert in range(EXPERTS):
        chosen = expert_ids == expert
        indices = jnp.nonzero(chosen, size=capacity, fill_value=0)[0].astype(jnp.int32)
        in_range = jnp.arange(capacity, dtype=jnp.int32) < jnp.sum(chosen.astype(jnp.int32))
        selected = normed[indices // 2]
        gate_part = jnp.dot(selected, gate_weight[expert], preferred_element_type=jnp.float32)
        up_part = jnp.dot(selected, up_weight[expert], preferred_element_type=jnp.float32)
        activation = (jax.nn.silu(gate_part) * up_part).astype(jnp.bfloat16)
        accumulated = jnp.zeros((capacity, D), jnp.float32)
        for block_index in range(N_EXPERT):
            lower = block_index * UNITS_DEV
            block_sum = jnp.dot(activation[:, lower:lower + UNITS_DEV], down_weight[expert, lower:lower + UNITS_DEV], preferred_element_type=jnp.float32)
            accumulated = accumulated + lax.optimization_barrier(block_sum.astype(jnp.bfloat16)).astype(jnp.float32)
        expert_out = accumulated.astype(jnp.bfloat16).astype(jnp.float32)
        collected = collected.at[indices].add(jnp.where(in_range[:, None], expert_out, jnp.float32(0.0)))
    collected = collected.reshape(TOKENS, 2, D)
    return hidden_state + route_weights[:, 0:1] * collected[:, 0] + route_weights[:, 1:2] * collected[:, 1]
```

```python
import functools

import jax
import jax.numpy as jnp
from jax import lax
from jax.experimental import pallas as pl
from jax.experimental.pallas import tpu as pltpu
from jax.sharding import PartitionSpec as P

MOST = 16
EPSILON = 1e-06
LANES = 128
TILE = 256
WIDE = 768
SLOTS = 3
MESH = pl.DeviceIdType.MESH
BF16 = jnp.bfloat16
F32 = jnp.float32


def dot(a, b):
    return jnp.dot(a, b, preferred_element_type=F32)


def kernel(
    sizes,
    attn_ref,
    residual_ref,
    proj_ref,
    gain_ref,
    gate_ref,
    up_ref,
    down_ref,
    meta_ref,
    out_ref,
    picked,
    gates,
    ups,
    downs,
    shared,
    psend,
    precv,
    hidden,
    gathered,
    metas,
    place,
    comb,
    scale,
    rows,
    act,
    block,
    part,
    sib,
    ssend,
    rrecv,
    pick_sem,
    proj_sem,
    gate_sem,
    up_sem,
    down_sem,
    meta_send,
    meta_recv,
    part_send,
    part_recv,
    row_send,
    row_recv,
    fwd_send,
    fwd_recv,
    sib_send,
    sib_recv,
    ret_send,
    ret_recv,
):
    mp, ex, rc, nl, depth, chunks = sizes
    group, half, pairs = mp * ex, mp * ex // 2, ex // 2
    units = gate_ref.shape[2]
    feats = residual_ref.shape[1]
    total = group * rc
    slots = group * MOST
    m, e = lax.axis_index("mp"), lax.axis_index("expert")
    g = m * ex + e
    c = lax.rem(e, 2)
    h = lax.div(g, 2)
    sibling = {"expert": e + 1 - 2 * c}

    def peer(index):
        return {"mp": lax.div(index, ex), "expert": lax.rem(index, ex)}

    picks = []
    for d in range(mp):
        owner = lax.rem(m + d, mp) * ex + e
        picks.append(
            pltpu.make_async_copy(
                attn_ref.at[pl.ds(pl.multiple_of(owner * rc, rc), rc), :],
                picked.at[pl.ds(d * rc, rc), :],
                pick_sem.at[d],
            )
        )
    projs = [
        pltpu.make_async_copy(
            proj_ref.at[:, pl.ds(j * WIDE, WIDE)],
            shared.at[pl.ds(0, depth), pl.ds(j * WIDE, WIDE)],
            proj_sem.at[j],
        )
        for j in range(chunks)
    ]
    gate_in = [
        pltpu.make_async_copy(gate_ref.at[l], gates.at[l % SLOTS], gate_sem.at[l])
        for l in range(nl)
    ]
    up_in = [
        pltpu.make_async_copy(up_ref.at[l], ups.at[l % SLOTS], up_sem.at[l]) for l in range(nl)
    ]

    def down_at(l):
        return shared.at[pl.ds(0, units), :] if l == nl - 1 else downs.at[l]

    down_in = [
        pltpu.make_async_copy(down_ref.at[l], down_at(l), down_sem.at[l]) for l in range(nl)
    ]
    for copy in picks + projs:
        copy.start()

    barrier = pltpu.get_barrier_semaphore()
    for d in range(1, group):
        pl.semaphore_signal(
            barrier, inc=1, device_id=peer(lax.rem(g + d, group)), device_id_type=MESH
        )
    pl.semaphore_wait(barrier, group - 1)

    metas[g] = meta_ref[...]
    meta_out = [
        pltpu.make_async_remote_copy(
            src_ref=meta_ref,
            dst_ref=metas.at[g],
            send_sem=meta_send.at[d - 1],
            recv_sem=meta_recv.at[d - 1],
            device_id=peer(lax.rem(g + d, group)),
            device_id_type=MESH,
        )
        for d in range(1, group)
    ]
    for copy in meta_out:
        copy.start()
    for copy in picks:
        copy.wait()

    part_out = []
    for j in range(chunks):
        projs[j].wait()
        if j == 0:
            for l in range(min(SLOTS, nl)):
                gate_in[l].start()
                up_in[l].start()
            for l in range(nl - 1):
                down_in[l].start()
        cols = pl.ds(j * WIDE, WIDE)
        value = dot(picked[...], shared[pl.ds(0, depth), cols])
        hidden[:, cols] = residual_ref[:, cols] + value[0:rc]
        for d in range(1, mp):
            psend[j, d - 1] = value[d * rc : (d + 1) * rc].astype(BF16)
            copy = pltpu.make_async_remote_copy(
                src_ref=psend.at[j, d - 1],
                dst_ref=precv.at[j, d - 1],
                send_sem=part_send.at[j, d - 1],
                recv_sem=part_recv.at[j, d - 1],
                device_id={"mp": lax.rem(m + d, mp)},
                device_id_type=MESH,
            )
            copy.start()
            part_out.append((j, d, copy))
    down_in[nl - 1].start()

    for copy in meta_out:
        copy.wait_recv()
    per = LANES // rc
    lanes = []
    for q in range(group // per):
        merged = metas[q * per]
        for i in range(1, per):
            merged = merged + metas[q * per + i]
        lanes.append(merged)
    table = jnp.concatenate(lanes, axis=1)
    first, second = table[0:1], table[1:2]
    ids = (lax.broadcasted_iota(jnp.int32, (16, total), 0) + m * nl).astype(F32)
    is_first = first == ids
    named = jnp.where(is_first, 1.0, jnp.where(second == ids, 1.0, 0.0))
    weight = jnp.where(is_first, table[2:3], table[3:4])
    row_at = lax.broadcasted_iota(jnp.int32, (total, total), 0)
    col_at = lax.broadcasted_iota(jnp.int32, (total, total), 1)
    earlier = jnp.where((row_at // rc == col_at // rc) & (row_at < col_at), 1.0, 0.0)
    rank = dot(named.astype(BF16), earlier.astype(BF16))
    base = (lax.broadcasted_iota(jnp.int32, (16, total), 1) // rc * MOST).astype(F32)
    target = jnp.where(named > 0.5, rank + base, -1.0)
    slot_at = lax.broadcasted_iota(jnp.int32, (slots, total), 0).astype(F32)
    for l in range(nl):
        hit = jnp.where(slot_at == target[l : l + 1], 1.0, 0.0)
        here = pl.ds(l * slots, slots)
        place[here, :] = hit.astype(BF16)
        comb[:, here] = hit.T.astype(BF16)
        scale[here, :] = jnp.sum(hit * weight[l : l + 1], axis=1, keepdims=True)

    for j, d, copy in part_out:
        copy.wait_recv()
        cols = pl.ds(j * WIDE, WIDE)
        hidden[:, cols] = hidden[:, cols] + precv[j, d - 1].astype(F32)
    state = hidden[...]
    inverse = lax.rsqrt(jnp.mean(state * state, axis=1, keepdims=True) + EPSILON)
    gathered[g] = (state * inverse * gain_ref[...]).astype(BF16)

    row_out = []
    for d in range(1, half):
        row_out.append(
            pltpu.make_async_remote_copy(
                src_ref=gathered.at[g],
                dst_ref=gathered.at[g],
                send_sem=row_send.at[d - 1],
                recv_sem=row_recv.at[d - 1],
                device_id=peer(2 * lax.rem(h + d, half) + c),
                device_id_type=MESH,
            )
        )
        row_out[-1].start()
    fwd_out = []
    for d in range(half):
        if d > 0:
            row_out[d - 1].wait_recv()
        source = 2 * lax.rem(h + half - d, half) + c
        fwd_out.append(
            pltpu.make_async_remote_copy(
                src_ref=gathered.at[source],
                dst_ref=gathered.at[source],
                send_sem=fwd_send.at[d],
                recv_sem=fwd_recv.at[d],
                device_id=sibling,
                device_id_type=MESH,
            )
        )
        fwd_out[-1].start()
    for copy in fwd_out:
        copy.wait_recv()

    @pl.loop(0, feats // TILE)
    def _(t):
        cols = pl.ds(pl.multiple_of(t * TILE, TILE), TILE)
        source = gathered[:, :, cols].reshape(total, TILE)
        rows[:, cols] = dot(place[...], source).astype(BF16)

    for l in range(nl):
        gate_in[l].wait()
        up_in[l].wait()
        here = pl.ds(l * slots, slots)

        @pl.loop(0, units // TILE)
        def _(t):
            cols = pl.ds(pl.multiple_of(t * TILE, TILE), TILE)
            gate = dot(rows[here, :], gates[l % SLOTS, :, cols])
            up = dot(rows[here, :], ups[l % SLOTS, :, cols])
            act[here, cols] = (gate / (1.0 + jnp.exp(-gate)) * up).astype(BF16)

        if l + SLOTS < nl:
            gate_in[l + SLOTS].start()
            up_in[l + SLOTS].start()

    for copy in down_in:
        copy.wait()

    sib_out, ret_out = [], []

    def pass_on(j):
        sib_out[j].wait_recv()
        ssend[j] = (part[j, c].astype(F32) + sib[j].astype(F32)).astype(BF16)
        for d in range(1, half):
            copy = pltpu.make_async_remote_copy(
                src_ref=ssend.at[j, lax.rem(h + d, half)],
                dst_ref=rrecv.at[j, d - 1],
                send_sem=ret_send.at[j, d - 1],
                recv_sem=ret_recv.at[j, d - 1],
                device_id=peer(2 * lax.rem(h + d, half) + c),
                device_id_type=MESH,
            )
            copy.start()
            ret_out.append((j, d, copy))

    for j in range(chunks):

        @pl.loop(0, WIDE // TILE)
        def _(t):
            to = pl.ds(pl.multiple_of(t * TILE, TILE), TILE)
            cols = pl.ds(pl.multiple_of(j * WIDE + t * TILE, TILE), TILE)
            for l in range(nl):
                here = pl.ds(l * slots, slots)
                matrix = shared[pl.ds(0, units), cols] if l == nl - 1 else downs[l, :, cols]
                block[here, :] = (dot(act[here, :], matrix) * scale[here, :]).astype(BF16)
            mixed = dot(comb[...], block[...]).astype(BF16)
            for index in range(group):
                part[j, index % 2, index // 2, :, to] = mixed[index * rc : (index + 1) * rc]

        copy = pltpu.make_async_remote_copy(
            src_ref=part.at[j, 1 - c],
            dst_ref=sib.at[j],
            send_sem=sib_send.at[j],
            recv_sem=sib_recv.at[j],
            device_id=sibling,
            device_id_type=MESH,
        )
        copy.start()
        sib_out.append(copy)
        if j > 0:
            pass_on(j - 1)
    pass_on(chunks - 1)

    for j in range(chunks):
        cols = pl.ds(j * WIDE, WIDE)
        value = ssend[j, h].astype(F32)
        for at, d, copy in ret_out:
            if at == j:
                copy.wait_recv()
                value = value + rrecv[j, d - 1].astype(F32)
        out_ref[:, cols] = hidden[:, cols] + value

    for copy in meta_out + row_out + fwd_out + sib_out:
        copy.wait_send()
    for _, _, copy in part_out + ret_out:
        copy.wait_send()


def body(
    attn_out,
    residual,
    proj_weight,
    norm_gain,
    gate_weight,
    up_weight,
    down_weight,
    routes,
    route_weights,
):
    mp = lax.axis_size("mp")
    ex = lax.axis_size("expert")
    rc, feats = residual.shape
    nl, _, units = gate_weight.shape
    depth = proj_weight.shape[0]
    group, half = mp * ex, mp * ex // 2
    total, slots = group * rc, nl * group * MOST
    chunks = feats // WIDE
    per = LANES // rc
    index = lax.axis_index("mp") * ex + lax.axis_index("expert")
    pairs = jnp.concatenate([routes.astype(F32), route_weights], axis=1).T
    meta = lax.dynamic_update_slice(
        jnp.zeros((8, LANES), F32), pairs, (jnp.int32(0), lax.rem(index, per) * rc)
    )
    vmem = pl.BlockSpec(memory_space=pltpu.VMEM)
    hbm = pl.BlockSpec(memory_space=pl.ANY)
    dma = pltpu.SemaphoreType.DMA
    return pl.pallas_call(
        functools.partial(kernel, (mp, ex, rc, nl, depth, chunks)),
        out_shape=jax.ShapeDtypeStruct((rc, feats), F32),
        in_specs=[hbm, vmem, hbm, vmem, hbm, hbm, hbm, vmem],
        out_specs=vmem,
        scratch_shapes=[
            pltpu.VMEM((mp * rc, depth), BF16),
            pltpu.VMEM((min(SLOTS, nl), feats, units), BF16),
            pltpu.VMEM((min(SLOTS, nl), feats, units), BF16),
            pltpu.VMEM((max(nl - 1, 1), units if nl > 1 else 16, feats), BF16),
            pltpu.VMEM((max(depth, units), feats), BF16),
            pltpu.VMEM((chunks, mp - 1, rc, WIDE), BF16),
            pltpu.VMEM((chunks, mp - 1, rc, WIDE), BF16),
            pltpu.VMEM((rc, feats), F32),
            pltpu.VMEM((group, rc, feats), BF16),
            pltpu.VMEM((group, 8, LANES), F32),
            pltpu.VMEM((slots, total), BF16),
            pltpu.VMEM((total, slots), BF16),
            pltpu.VMEM((slots, 1), F32),
            pltpu.VMEM((slots, feats), BF16),
            pltpu.VMEM((slots, units), BF16),
            pltpu.VMEM((slots, TILE), BF16),
            pltpu.VMEM((chunks, 2, half, rc, WIDE), BF16),
            pltpu.VMEM((chunks, half, rc, WIDE), BF16),
            pltpu.VMEM((chunks, half, rc, WIDE), BF16),
            pltpu.VMEM((chunks, half - 1, rc, WIDE), BF16),
            dma((mp,)),
            dma((chunks,)),
            dma((nl,)),
            dma((nl,)),
            dma((nl,)),
            dma((group - 1,)),
            dma((group - 1,)),
            dma((chunks, mp - 1)),
            dma((chunks, mp - 1)),
            dma((half - 1,)),
            dma((half - 1,)),
            dma((half,)),
            dma((half,)),
            dma((chunks,)),
            dma((chunks,)),
            dma((chunks, half - 1)),
            dma((chunks, half - 1)),
        ],
        compiler_params=pltpu.CompilerParams(
            collective_id=0, has_side_effects=True, vmem_limit_bytes=62 * 1024 * 1024
        ),
    )(
        attn_out,
        residual,
        proj_weight,
        norm_gain.reshape(1, feats),
        gate_weight,
        up_weight,
        down_weight,
        meta,
    )


def solution(mesh):
    in_specs = (
        P("dp", "mp"),
        P(("dp", "mp", "expert"), None),
        P("mp", None),
        P(),
        P("mp", None, "expert"),
        P("mp", None, "expert"),
        P("mp", "expert", None),
        P(("dp", "mp", "expert"), None),
        P(("dp", "mp", "expert"), None),
    )
    out_specs = P(("dp", "mp", "expert"), None)
    return jax.shard_map(body, mesh=mesh, in_specs=in_specs, out_specs=out_specs, check_vma=False)
```

```python
import functools

import jax
import jax.numpy as jnp
from jax import lax
from jax.experimental import pallas as pl
from jax.experimental.pallas import tpu as pltpu
from jax.sharding import PartitionSpec as P

MOST = 16
EPSILON = 1e-06
LANES = 128
TILE = 256
WIDE = 768
MESH = pl.DeviceIdType.MESH
BF16 = jnp.bfloat16
F32 = jnp.float32


def dot(a, b):
    return jnp.dot(a, b, preferred_element_type=F32)


def kernel(
    sizes,
    attn_ref,
    residual_ref,
    proj_ref,
    gain_ref,
    gate_ref,
    up_ref,
    down_ref,
    routes_ref,
    weights_ref,
    out_ref,
    picked,
    res,
    gate_big,
    up_big,
    gate_small,
    up_small,
    down_small,
    proj,
    psend,
    precv,
    psum,
    gathered0,
    gathered1,
    gathered2,
    metas,
    place,
    comb,
    rows,
    gate_acc,
    up_acc,
    act,
    block,
    part32,
    part,
    sib,
    ssend,
    rrecv,
    pick_sem,
    res_sem,
    proj_sem,
    gate_sem,
    up_sem,
    down_sem,
    meta_send,
    meta_recv,
    part_send,
    part_recv,
    row_send,
    row_recv,
    fwd_send,
    fwd_recv,
    sib_send,
    sib_recv,
    ret_send,
    ret_recv,
):
    mp, ex, rc, nl = sizes
    group, half = mp * ex, mp * ex // 2
    units = gate_ref.shape[2]
    feats = residual_ref.shape[1]
    rest = feats - 2 * units
    spans = [(0, units), (units, units), (2 * units, rest)]
    gathered = [gathered0, gathered1, gathered2]
    total = group * rc
    slots = group * MOST
    m, e = lax.axis_index("mp"), lax.axis_index("expert")
    g = m * ex + e
    c = lax.rem(e, 2)
    h = lax.div(g, 2)
    sibling = {"expert": e + 1 - 2 * c}

    def peer(index):
        return {"mp": lax.div(index, ex), "expert": lax.rem(index, ex)}

    def remote(src, dst, send, recv, to):
        return pltpu.make_async_remote_copy(
            src_ref=src, dst_ref=dst, send_sem=send, recv_sem=recv, device_id=to, device_id_type=MESH
        )

    picks = []
    for d in range(mp):
        owner = lax.rem(m + d, mp) * ex + e
        picks.append(
            pltpu.make_async_copy(
                attn_ref.at[pl.ds(pl.multiple_of(owner * rc, rc), rc), :],
                picked.at[pl.ds(d * rc, rc), :],
                pick_sem.at[d],
            )
        )
    projs = [
        pltpu.make_async_copy(
            proj_ref.at[:, pl.ds(j * WIDE, WIDE)], proj.at[:, pl.ds(j * WIDE, WIDE)], proj_sem.at[j]
        )
        for j in range(feats // WIDE)
    ]
    res_in = pltpu.make_async_copy(residual_ref, res, res_sem)

    def gate_at(l, k):
        return gate_small.at[l] if k == 2 else gate_big.at[l, k]

    def up_at(l, k):
        return up_small.at[l] if k == 2 else up_big.at[l, k]

    def down_at(l, k):
        return (gate_big.at[l, 0], up_big.at[l, 0], down_small.at[l])[k]

    def load(ref, to, sem, l, k):
        start, size = spans[k]
        return pltpu.make_async_copy(ref.at[l, pl.ds(start, size), :], to(l, k), sem.at[l, k])

    experts = range(nl)
    gate_in = [[load(gate_ref, gate_at, gate_sem, l, k) for k in range(3)] for l in experts]
    up_in = [[load(up_ref, up_at, up_sem, l, k) for k in range(3)] for l in experts]
    down_in = [
        [
            pltpu.make_async_copy(
                down_ref.at[l, :, pl.ds(spans[k][0], spans[k][1])],
                down_at(l, k),
                down_sem.at[l, k],
            )
            for k in range(3)
        ]
        for l in experts
    ]
    for copy in picks + projs + [res_in]:
        copy.start()

    barrier = pltpu.get_barrier_semaphore()
    for d in range(1, group):
        pl.semaphore_signal(
            barrier, inc=1, device_id=peer(lax.rem(g + d, group)), device_id_type=MESH
        )

    per = LANES // rc
    lane = lax.broadcasted_iota(jnp.int32, (2, LANES), 1)
    mine = lane // rc == lax.rem(g, per)
    lines = [
        jnp.where(mine, jnp.concatenate([value] * per, axis=1), 0.0)
        for value in (routes_ref[...].astype(F32), weights_ref[...])
    ]
    metas[g] = jnp.concatenate(lines + [jnp.zeros((4, LANES), F32)], axis=0)
    pl.semaphore_wait(barrier, group - 1)

    meta_out = [
        remote(
            metas.at[g],
            metas.at[g],
            meta_send.at[d - 1],
            meta_recv.at[d - 1],
            peer(lax.rem(g + d, group)),
        )
        for d in range(1, group)
    ]
    for copy in meta_out:
        copy.start()
    for copy in picks:
        copy.wait()

    part_out = []
    for j in range(feats // WIDE):
        projs[j].wait()
        if j == 0:
            for k in range(3):
                for l in experts:
                    gate_in[l][k].start()
                    up_in[l][k].start()
            for l in experts:
                down_in[l][2].start()
        cols = pl.ds(j * WIDE, WIDE)
        value = dot(picked[...], proj[:, cols])
        psum[:, cols] = value[0:rc]
        for d in range(1, mp):
            psend[j, d - 1] = value[d * rc : (d + 1) * rc].astype(BF16)
            copy = remote(
                psend.at[j, d - 1],
                precv.at[j, d - 1],
                part_send.at[j, d - 1],
                part_recv.at[j, d - 1],
                {"mp": lax.rem(m + d, mp)},
            )
            copy.start()
            part_out.append((j, d, copy))

    for copy in meta_out:
        copy.wait_recv()
    lanes = []
    for q in range(group // per):
        merged = metas[q * per]
        for i in range(1, per):
            merged = merged + metas[q * per + i]
        lanes.append(merged)
    table = jnp.concatenate(lanes, axis=1)
    first, second = table[0:1], table[1:2]
    ids = (lax.broadcasted_iota(jnp.int32, (16, total), 0) + m * nl).astype(F32)
    is_first = first == ids
    named = jnp.where(is_first, 1.0, jnp.where(second == ids, 1.0, 0.0))
    weight = jnp.where(is_first, table[2:3], table[3:4])
    row_at = lax.broadcasted_iota(jnp.int32, (total, total), 0)
    col_at = lax.broadcasted_iota(jnp.int32, (total, total), 1)
    earlier = jnp.where((row_at // rc == col_at // rc) & (row_at < col_at), 1.0, 0.0)
    rank = dot(named.astype(BF16), earlier.astype(BF16))
    base = (lax.broadcasted_iota(jnp.int32, (16, total), 1) // rc * MOST).astype(F32)
    target = jnp.where(named > 0.5, rank + base, -1.0)
    slot_at = lax.broadcasted_iota(jnp.int32, (slots, total), 0).astype(F32)
    for l in experts:
        hit = slot_at == target[l : l + 1]
        here = pl.ds(l * slots, slots)
        place[here, :] = jnp.where(hit, 1.0, 0.0).astype(BF16)
        share = jnp.where(hit, weight[l : l + 1], 0.0).T
        high = share.astype(BF16)
        comb[pl.ds(0, total), here] = high
        comb[pl.ds(total, total), here] = (share - high.astype(F32)).astype(BF16)

    res_in.wait()
    for j, d, copy in part_out:
        copy.wait_recv()
        cols = pl.ds(j * WIDE, WIDE)
        psum[:, cols] = psum[:, cols] + precv[j, d - 1].astype(F32)
    state = res[...] + psum[...]
    inverse = lax.rsqrt(jnp.mean(state * state, axis=1, keepdims=True) + EPSILON)
    normed = (state * inverse * gain_ref[...].reshape(1, feats)).astype(BF16)

    row_out, fwd_out = [], []
    for k, (start, size) in enumerate(spans):
        gathered[k][g] = normed[:, start : start + size]
        row_out.append([])
        for d in range(1, half):
            row_out[k].append(
                remote(
                    gathered[k].at[g],
                    gathered[k].at[g],
                    row_send.at[k, d - 1],
                    row_recv.at[k, d - 1],
                    peer(2 * lax.rem(h + d, half) + c),
                )
            )
            row_out[k][-1].start()
        fwd_out.append([])
        for d in range(half):
            source = 2 * lax.rem(h + half - d, half) + c
            fwd_out[k].append(
                remote(
                    gathered[k].at[source],
                    gathered[k].at[source],
                    fwd_send.at[k, d],
                    fwd_recv.at[k, d],
                    sibling,
                )
            )
        fwd_out[k][0].start()

    def forward(k):
        for d in range(1, half):
            row_out[k][d - 1].wait_recv()
            fwd_out[k][d].start()

    forward(0)
    for k, (start, size) in enumerate(spans):
        for copy in fwd_out[k]:
            copy.wait_recv()

        @pl.loop(0, size // TILE)
        def _(t):
            cols = pl.ds(pl.multiple_of(t * TILE, TILE), TILE)
            rows[:, cols] = dot(place[...], gathered[k][:, :, cols].reshape(total, TILE)).astype(BF16)

        for l in experts:
            gate_in[l][k].wait()
            up_in[l][k].wait()
            here = pl.ds(l * slots, slots)

            @pl.loop(0, units // TILE)
            def _(t):
                cols = pl.ds(pl.multiple_of(t * TILE, TILE), TILE)
                left = rows[here, pl.ds(0, size)]
                gate = dot(left, gate_at(l, k)[:, cols])
                up = dot(left, up_at(l, k)[:, cols])
                if k > 0:
                    gate = gate + gate_acc[here, cols]
                    up = up + up_acc[here, cols]
                if k < 2:
                    gate_acc[here, cols] = gate
                    up_acc[here, cols] = up
                else:
                    act[here, cols] = (gate / (1.0 + jnp.exp(-gate)) * up).astype(BF16)

            if k == 0:
                down_in[l][0].start()
                down_in[l][1].start()
            if k < 2 and l == max(nl - 2, 0):
                forward(k + 1)

    sib_out, ret_out = [], []

    def pass_on(j):
        cols = pl.ds(j * TILE, TILE)
        sib_out[j].wait_recv()
        value = part32[j % 2, c] + sib[j].astype(F32)
        ssend[j] = value.astype(BF16)
        out_ref[:, cols] = psum[:, cols] + (part32[j % 2, c, h] + sib[j, h].astype(F32))
        for d in range(1, half):
            copy = remote(
                ssend.at[j, lax.rem(h + d, half)],
                rrecv.at[j, d - 1],
                ret_send.at[j, d - 1],
                ret_recv.at[j, d - 1],
                peer(2 * lax.rem(h + d, half) + c),
            )
            copy.start()
            ret_out.append((j, d, copy))

    chunks = feats // TILE
    for j in range(chunks):
        k = min(j * TILE // units, 2)
        inside = pl.ds(j * TILE - spans[k][0], TILE)
        for l in experts:
            if j * TILE == spans[k][0]:
                down_in[l][k].wait()
            here = pl.ds(l * slots, slots)
            block[here, :] = dot(act[here, :], down_at(l, k)[:, inside]).astype(BF16)
        both = dot(comb[...], block[...])
        mixed = both[0:total] + both[total : 2 * total]
        for index in range(group):
            one = mixed[index * rc : (index + 1) * rc]
            part32[j % 2, index % 2, index // 2] = one
            part[j, index % 2, index // 2] = one.astype(BF16)
        copy = remote(part.at[j, 1 - c], sib.at[j], sib_send.at[j], sib_recv.at[j], sibling)
        copy.start()
        sib_out.append(copy)
        if j > 0:
            pass_on(j - 1)
    pass_on(chunks - 1)

    for j, d, copy in ret_out:
        cols = pl.ds(j * TILE, TILE)
        copy.wait_recv()
        out_ref[:, cols] = out_ref[:, cols] + rrecv[j, d - 1].astype(F32)

    for copy in meta_out + sib_out + sum(row_out, []) + sum(fwd_out, []):
        copy.wait_send()
    for _, _, copy in part_out + ret_out:
        copy.wait_send()


def body(
    attn_out,
    residual,
    proj_weight,
    norm_gain,
    gate_weight,
    up_weight,
    down_weight,
    routes,
    route_weights,
):
    mp = lax.axis_size("mp")
    ex = lax.axis_size("expert")
    rc, feats = residual.shape
    nl, _, units = gate_weight.shape
    depth = proj_weight.shape[0]
    group, half = mp * ex, mp * ex // 2
    total, slots = group * rc, nl * group * MOST
    wide, chunks = feats // WIDE, feats // TILE
    rest = feats - 2 * units
    vmem = pl.BlockSpec(memory_space=pltpu.VMEM)
    hbm = pl.BlockSpec(memory_space=pl.ANY)
    dma = pltpu.SemaphoreType.DMA
    added = pl.pallas_call(
        functools.partial(kernel, (mp, ex, rc, nl)),
        out_shape=jax.ShapeDtypeStruct((rc, feats), F32),
        in_specs=[hbm, hbm, hbm, vmem, hbm, hbm, hbm, vmem, vmem],
        out_specs=vmem,
        scratch_shapes=[
            pltpu.VMEM((mp * rc, depth), BF16),
            pltpu.VMEM((rc, feats), F32),
            pltpu.VMEM((nl, 2, units, units), BF16),
            pltpu.VMEM((nl, 2, units, units), BF16),
            pltpu.VMEM((nl, rest, units), BF16),
            pltpu.VMEM((nl, rest, units), BF16),
            pltpu.VMEM((nl, units, rest), BF16),
            pltpu.VMEM((depth, feats), BF16),
            pltpu.VMEM((wide, mp - 1, rc, WIDE), BF16),
            pltpu.VMEM((wide, mp - 1, rc, WIDE), BF16),
            pltpu.VMEM((rc, feats), F32),
            pltpu.VMEM((group, rc, units), BF16),
            pltpu.VMEM((group, rc, units), BF16),
            pltpu.VMEM((group, rc, rest), BF16),
            pltpu.VMEM((group, 8, LANES), F32),
            pltpu.VMEM((slots, total), BF16),
            pltpu.VMEM((2 * total, slots), BF16),
            pltpu.VMEM((slots, units), BF16),
            pltpu.VMEM((slots, units), F32),
            pltpu.VMEM((slots, units), F32),
            pltpu.VMEM((slots, units), BF16),
            pltpu.VMEM((slots, TILE), BF16),
            pltpu.VMEM((2, 2, half, rc, TILE), F32),
            pltpu.VMEM((chunks, 2, half, rc, TILE), BF16),
            pltpu.VMEM((chunks, half, rc, TILE), BF16),
            pltpu.VMEM((chunks, half, rc, TILE), BF16),
            pltpu.VMEM((chunks, half - 1, rc, TILE), BF16),
            dma((mp,)),
            dma(()),
            dma((wide,)),
            dma((nl, 3)),
            dma((nl, 3)),
            dma((nl, 3)),
            dma((group - 1,)),
            dma((group - 1,)),
            dma((wide, mp - 1)),
            dma((wide, mp - 1)),
            dma((3, half - 1)),
            dma((3, half - 1)),
            dma((3, half)),
            dma((3, half)),
            dma((chunks,)),
            dma((chunks,)),
            dma((chunks, half - 1)),
            dma((chunks, half - 1)),
        ],
        compiler_params=pltpu.CompilerParams(
            collective_id=0, has_side_effects=True, vmem_limit_bytes=62 * 1024 * 1024
        ),
    )(
        attn_out,
        residual,
        proj_weight,
        norm_gain,
        gate_weight,
        up_weight,
        down_weight,
        routes.T,
        route_weights.T,
    )
    return added + residual


def solution(mesh):
    in_specs = (
        P("dp", "mp"),
        P(("dp", "mp", "expert"), None),
        P("mp", None),
        P(),
        P("mp", None, "expert"),
        P("mp", None, "expert"),
        P("mp", "expert", None),
        P(("dp", "mp", "expert"), None),
        P(("dp", "mp", "expert"), None),
    )
    out_specs = P(("dp", "mp", "expert"), None)
    return jax.shard_map(body, mesh=mesh, in_specs=in_specs, out_specs=out_specs, check_vma=False)
```

```python
import functools

import jax
import jax.numpy as jnp
from jax import lax
from jax.experimental import pallas as pl
from jax.experimental.pallas import tpu as pltpu
from jax.sharding import PartitionSpec as P

MOST = 16
EPSILON = 1e-06
LANES = 128
TILE = 256
WIDE = 768
LAG = 3
MESH = pl.DeviceIdType.MESH
BF16 = jnp.bfloat16
F32 = jnp.float32


def dot(a, b):
    return jnp.dot(a, b, preferred_element_type=F32)


def kernel(
    sizes,
    attn_ref,
    residual_ref,
    proj_ref,
    gain_ref,
    gate_ref,
    up_ref,
    down_ref,
    routes_ref,
    weights_ref,
    out_ref,
    picked,
    res,
    gate_big,
    up_big,
    gate_small,
    up_small,
    down_small,
    proj,
    psend,
    precv,
    psum,
    gathered0,
    gathered1,
    gathered2,
    metas,
    place,
    comb,
    rows,
    gate_acc,
    up_acc,
    act,
    block,
    part32,
    part,
    sib,
    ssend,
    rrecv,
    pick_sem,
    res_sem,
    proj_sem,
    gate_sem,
    up_sem,
    down_sem,
    meta_send,
    meta_recv,
    part_send,
    part_recv,
    row_send,
    row_recv,
    fwd_send,
    fwd_recv,
    sib_send,
    sib_recv,
    ret_send,
    ret_recv,
):
    mp, ex, rc, nl = sizes
    group, half = mp * ex, mp * ex // 2
    units = gate_ref.shape[2]
    feats = residual_ref.shape[1]
    rest = feats - 2 * units
    spans = [(0, units), (units, units), (2 * units, rest)]
    gathered = [gathered0, gathered1, gathered2]
    total = group * rc
    slots = group * MOST
    m, e = lax.axis_index("mp"), lax.axis_index("expert")
    g = m * ex + e
    c = lax.rem(e, 2)
    h = lax.div(g, 2)
    sibling = {"expert": e + 1 - 2 * c}

    def peer(index):
        return {"mp": lax.div(index, ex), "expert": lax.rem(index, ex)}

    def remote(src, dst, send, recv, to):
        return pltpu.make_async_remote_copy(
            src_ref=src, dst_ref=dst, send_sem=send, recv_sem=recv, device_id=to, device_id_type=MESH
        )

    picks = []
    for d in range(mp):
        owner = lax.rem(m + d, mp) * ex + e
        picks.append(
            pltpu.make_async_copy(
                attn_ref.at[pl.ds(pl.multiple_of(owner * rc, rc), rc), :],
                picked.at[pl.ds(d * rc, rc), :],
                pick_sem.at[d],
            )
        )
    projs = [
        pltpu.make_async_copy(
            proj_ref.at[:, pl.ds(j * WIDE, WIDE)], proj.at[:, pl.ds(j * WIDE, WIDE)], proj_sem.at[j]
        )
        for j in range(feats // WIDE)
    ]
    res_in = pltpu.make_async_copy(residual_ref, res, res_sem)

    def gate_at(l, k):
        return gate_small.at[l] if k == 2 else gate_big.at[l, k]

    def up_at(l, k):
        return up_small.at[l] if k == 2 else up_big.at[l, k]

    def down_at(l, k):
        return (gate_big.at[l, 0], up_big.at[l, 0], down_small.at[l])[k]

    def load(ref, to, sem, l, k):
        start, size = spans[k]
        return pltpu.make_async_copy(ref.at[l, pl.ds(start, size), :], to(l, k), sem.at[l, k])

    experts = range(nl)
    gate_in = [[load(gate_ref, gate_at, gate_sem, l, k) for k in range(3)] for l in experts]
    up_in = [[load(up_ref, up_at, up_sem, l, k) for k in range(3)] for l in experts]
    down_in = [
        [
            pltpu.make_async_copy(
                down_ref.at[l, :, pl.ds(spans[k][0], spans[k][1])],
                down_at(l, k),
                down_sem.at[l, k],
            )
            for k in range(3)
        ]
        for l in experts
    ]
    for copy in picks + projs + [res_in]:
        copy.start()

    barrier = pltpu.get_barrier_semaphore()
    for d in range(1, group):
        pl.semaphore_signal(
            barrier, inc=1, device_id=peer(lax.rem(g + d, group)), device_id_type=MESH
        )

    per = LANES // rc
    lane = lax.broadcasted_iota(jnp.int32, (2, LANES), 1)
    mine = lane // rc == lax.rem(g, per)
    lines = [
        jnp.where(mine, jnp.concatenate([value] * per, axis=1), 0.0)
        for value in (routes_ref[...].astype(F32), weights_ref[...])
    ]
    metas[g] = jnp.concatenate(lines + [jnp.zeros((4, LANES), F32)], axis=0)
    pl.semaphore_wait(barrier, group - 1)

    meta_out = [
        remote(
            metas.at[g],
            metas.at[g],
            meta_send.at[d - 1],
            meta_recv.at[d - 1],
            peer(lax.rem(g + d, group)),
        )
        for d in range(1, group)
    ]
    for copy in meta_out:
        copy.start()
    for copy in picks:
        copy.wait()

    part_out = []
    for j in range(feats // WIDE):
        projs[j].wait()
        if j == 0:
            for k in range(3):
                for l in experts:
                    gate_in[l][k].start()
                    up_in[l][k].start()
            for l in experts:
                down_in[l][2].start()
        cols = pl.ds(j * WIDE, WIDE)
        value = dot(picked[...], proj[:, cols])
        psum[:, cols] = value[0:rc]
        for d in range(1, mp):
            psend[j, d - 1] = value[d * rc : (d + 1) * rc].astype(BF16)
            copy = remote(
                psend.at[j, d - 1],
                precv.at[j, d - 1],
                part_send.at[j, d - 1],
                part_recv.at[j, d - 1],
                {"mp": lax.rem(m + d, mp)},
            )
            copy.start()
            part_out.append((j, d, copy))

    for copy in meta_out:
        copy.wait_recv()
    lanes = []
    for q in range(group // per):
        merged = metas[q * per]
        for i in range(1, per):
            merged = merged + metas[q * per + i]
        lanes.append(merged)
    table = jnp.concatenate(lanes, axis=1)
    first, second = table[0:1], table[1:2]
    ids = (lax.broadcasted_iota(jnp.int32, (16, total), 0) + m * nl).astype(F32)
    is_first = first == ids
    named = jnp.where(is_first, 1.0, jnp.where(second == ids, 1.0, 0.0))
    weight = jnp.where(is_first, table[2:3], table[3:4])
    row_at = lax.broadcasted_iota(jnp.int32, (total, total), 0)
    col_at = lax.broadcasted_iota(jnp.int32, (total, total), 1)
    earlier = jnp.where((row_at // rc == col_at // rc) & (row_at < col_at), 1.0, 0.0)
    rank = dot(named.astype(BF16), earlier.astype(BF16))
    base = (lax.broadcasted_iota(jnp.int32, (16, total), 1) // rc * MOST).astype(F32)
    target = jnp.where(named > 0.5, rank + base, -1.0)
    slot_at = lax.broadcasted_iota(jnp.int32, (slots, total), 0).astype(F32)
    for l in experts:
        hit = slot_at == target[l : l + 1]
        here = pl.ds(l * slots, slots)
        place[here, :] = jnp.where(hit, 1.0, 0.0).astype(BF16)
        share = jnp.where(hit, weight[l : l + 1], 0.0).T
        high = share.astype(BF16)
        comb[pl.ds(0, total), here] = high
        comb[pl.ds(total, total), here] = (share - high.astype(F32)).astype(BF16)

    res_in.wait()
    for j, d, copy in part_out:
        copy.wait_recv()
        cols = pl.ds(j * WIDE, WIDE)
        psum[:, cols] = psum[:, cols] + precv[j, d - 1].astype(F32)
    state = res[...] + psum[...]
    inverse = lax.rsqrt(jnp.mean(state * state, axis=1, keepdims=True) + EPSILON)
    normed = (state * inverse * gain_ref[...].reshape(1, feats)).astype(BF16)

    row_out, fwd_out = [], []
    for k, (start, size) in enumerate(spans):
        gathered[k][g] = normed[:, start : start + size]
        row_out.append([])
        for d in range(1, half):
            row_out[k].append(
                remote(
                    gathered[k].at[g],
                    gathered[k].at[g],
                    row_send.at[k, d - 1],
                    row_recv.at[k, d - 1],
                    peer(2 * lax.rem(h + d, half) + c),
                )
            )
            row_out[k][-1].start()
        fwd_out.append([])
        for d in range(half):
            source = 2 * lax.rem(h + half - d, half) + c
            fwd_out[k].append(
                remote(
                    gathered[k].at[source],
                    gathered[k].at[source],
                    fwd_send.at[k, d],
                    fwd_recv.at[k, d],
                    sibling,
                )
            )
        fwd_out[k][0].start()

    def forward(k):
        for d in range(1, half):
            row_out[k][d - 1].wait_recv()
            fwd_out[k][d].start()

    forward(0)

    def dispatch(k, at):
        for copy in fwd_out[k]:
            copy.wait_recv()

        @pl.loop(0, spans[k][1] // TILE)
        def _(t):
            cols = pl.ds(pl.multiple_of(t * TILE, TILE), TILE)
            to = pl.ds(pl.multiple_of(at + t * TILE, TILE), TILE)
            rows[:, to] = dot(place[...], gathered[k][:, :, cols].reshape(total, TILE)).astype(BF16)

    dispatch(0, 0)
    for l in experts:
        gate_in[l][0].wait()
        up_in[l][0].wait()
        here = pl.ds(l * slots, slots)

        @pl.loop(0, units // TILE)
        def _(t):
            cols = pl.ds(pl.multiple_of(t * TILE, TILE), TILE)
            left = rows[here, pl.ds(0, units)]
            gate_acc[here, cols] = dot(left, gate_big[l, 0, :, cols])
            up_acc[here, cols] = dot(left, up_big[l, 0, :, cols])

        down_in[l][0].start()
        down_in[l][1].start()
        if l == max(nl - 2, 0):
            forward(1)
            forward(2)

    dispatch(1, 0)
    dispatch(2, units)
    for l in experts:
        for k in (1, 2):
            gate_in[l][k].wait()
            up_in[l][k].wait()
        here = pl.ds(l * slots, slots)

        @pl.loop(0, units // TILE)
        def _(t):
            cols = pl.ds(pl.multiple_of(t * TILE, TILE), TILE)
            left = rows[here, pl.ds(0, units)]
            last = rows[here, pl.ds(units, rest)]
            gate = dot(left, gate_big[l, 1, :, cols]) + dot(last, gate_small[l, :, cols])
            up = dot(left, up_big[l, 1, :, cols]) + dot(last, up_small[l, :, cols])
            gate = gate + gate_acc[here, cols]
            up = up + up_acc[here, cols]
            act[here, cols] = (gate / (1.0 + jnp.exp(-gate)) * up).astype(BF16)

    def to_sibling(j):
        return remote(part.at[j, 1 - c], sib.at[j], sib_send.at[j], sib_recv.at[j], sibling)

    def to_owner(j, d):
        return remote(
            ssend.at[j, lax.rem(h + d, half)],
            rrecv.at[j, d - 1],
            ret_send.at[j, d - 1],
            ret_recv.at[j, d - 1],
            peer(2 * lax.rem(h + d, half) + c),
        )

    def columns(j):
        return pl.ds(pl.multiple_of(j * TILE, TILE), TILE)

    def pass_on(j):
        to_sibling(j).wait_recv()
        slot = lax.rem(j, LAG + 1)
        ssend[j] = (part32[slot, c] + sib[j].astype(F32)).astype(BF16)
        for d in range(1, half):
            to_owner(j, d).start()
        own = part32[slot, c, h] + sib[j, h].astype(F32)
        out_ref[:, columns(j)] = psum[:, columns(j)] + own

    chunks = feats // TILE
    for k, (start, size) in enumerate(spans):
        for l in experts:
            down_in[l][k].wait()

        @pl.loop(0, size // TILE)
        def _(t):
            j = start // TILE + t
            for l in experts:
                here = pl.ds(l * slots, slots)
                block[here, :] = dot(act[here, :], down_at(l, k)[:, columns(t)]).astype(BF16)
            both = dot(comb[...], block[...])
            mixed = both[0:total] + both[total : 2 * total]
            slot = lax.rem(j, LAG + 1)
            for index in range(group):
                one = mixed[index * rc : (index + 1) * rc]
                part32[slot, index % 2, index // 2] = one
                part[j, index % 2, index // 2] = one.astype(BF16)
            to_sibling(j).start()

            @pl.when(j >= LAG)
            def _():
                pass_on(j - LAG)

    @pl.loop(chunks - LAG, chunks)
    def _(j):
        pass_on(j)

    @pl.loop(0, chunks)
    def _(j):
        value = out_ref[:, columns(j)]
        for d in range(1, half):
            to_owner(j, d).wait_recv()
            value = value + rrecv[j, d - 1].astype(F32)
        out_ref[:, columns(j)] = value

    @pl.loop(0, chunks)
    def _(j):
        to_sibling(j).wait_send()
        for d in range(1, half):
            to_owner(j, d).wait_send()

    for copy in meta_out + sum(row_out, []) + sum(fwd_out, []):
        copy.wait_send()
    for _, _, copy in part_out:
        copy.wait_send()


def body(
    attn_out,
    residual,
    proj_weight,
    norm_gain,
    gate_weight,
    up_weight,
    down_weight,
    routes,
    route_weights,
):
    mp = lax.axis_size("mp")
    ex = lax.axis_size("expert")
    rc, feats = residual.shape
    nl, _, units = gate_weight.shape
    depth = proj_weight.shape[0]
    group, half = mp * ex, mp * ex // 2
    total, slots = group * rc, nl * group * MOST
    wide, chunks = feats // WIDE, feats // TILE
    rest = feats - 2 * units
    vmem = pl.BlockSpec(memory_space=pltpu.VMEM)
    hbm = pl.BlockSpec(memory_space=pl.ANY)
    dma = pltpu.SemaphoreType.DMA
    added = pl.pallas_call(
        functools.partial(kernel, (mp, ex, rc, nl)),
        out_shape=jax.ShapeDtypeStruct((rc, feats), F32),
        in_specs=[hbm, hbm, hbm, vmem, hbm, hbm, hbm, vmem, vmem],
        out_specs=vmem,
        scratch_shapes=[
            pltpu.VMEM((mp * rc, depth), BF16),
            pltpu.VMEM((rc, feats), F32),
            pltpu.VMEM((nl, 2, units, units), BF16),
            pltpu.VMEM((nl, 2, units, units), BF16),
            pltpu.VMEM((nl, rest, units), BF16),
            pltpu.VMEM((nl, rest, units), BF16),
            pltpu.VMEM((nl, units, rest), BF16),
            pltpu.VMEM((depth, feats), BF16),
            pltpu.VMEM((wide, mp - 1, rc, WIDE), BF16),
            pltpu.VMEM((wide, mp - 1, rc, WIDE), BF16),
            pltpu.VMEM((rc, feats), F32),
            pltpu.VMEM((group, rc, units), BF16),
            pltpu.VMEM((group, rc, units), BF16),
            pltpu.VMEM((group, rc, rest), BF16),
            pltpu.VMEM((group, 8, LANES), F32),
            pltpu.VMEM((slots, total), BF16),
            pltpu.VMEM((2 * total, slots), BF16),
            pltpu.VMEM((slots, units + rest), BF16),
            pltpu.VMEM((slots, units), F32),
            pltpu.VMEM((slots, units), F32),
            pltpu.VMEM((slots, units), BF16),
            pltpu.VMEM((slots, TILE), BF16),
            pltpu.VMEM((LAG + 1, 2, half, rc, TILE), F32),
            pltpu.VMEM((chunks, 2, half, rc, TILE), BF16),
            pltpu.VMEM((chunks, half, rc, TILE), BF16),
            pltpu.VMEM((chunks, half, rc, TILE), BF16),
            pltpu.VMEM((chunks, half - 1, rc, TILE), BF16),
            dma((mp,)),
            dma(()),
            dma((wide,)),
            dma((nl, 3)),
            dma((nl, 3)),
            dma((nl, 3)),
            dma((group - 1,)),
            dma((group - 1,)),
            dma((wide, mp - 1)),
            dma((wide, mp - 1)),
            dma((3, half - 1)),
            dma((3, half - 1)),
            dma((3, half)),
            dma((3, half)),
            dma((chunks,)),
            dma((chunks,)),
            dma((chunks, half - 1)),
            dma((chunks, half - 1)),
        ],
        compiler_params=pltpu.CompilerParams(
            collective_id=0, has_side_effects=True, vmem_limit_bytes=62 * 1024 * 1024
        ),
    )(
        attn_out,
        residual,
        proj_weight,
        norm_gain,
        gate_weight,
        up_weight,
        down_weight,
        routes.T,
        route_weights.T,
    )
    return added + residual


def solution(mesh):
    in_specs = (
        P("dp", "mp"),
        P(("dp", "mp", "expert"), None),
        P("mp", None),
        P(),
        P("mp", None, "expert"),
        P("mp", None, "expert"),
        P("mp", "expert", None),
        P(("dp", "mp", "expert"), None),
        P(("dp", "mp", "expert"), None),
    )
    out_specs = P(("dp", "mp", "expert"), None)
    return jax.shard_map(body, mesh=mesh, in_specs=in_specs, out_specs=out_specs, check_vma=False)
```
